32 devices in a mesh: lat: 8 (over y, x, core), scale: 4 (over z).
Axes of the slice: x: 2, y: 2, z: 4, core: 2. Of those that a mesh axis runs over, the one named last changes fastest.
Arguments:
- state: float32 [512, 2, 128, 512], P('lat', None, None, 'scale'), may hold values from -6 to 6
- noise: float32 [512, 2, 128, 512], P('lat', None, None, 'scale'), may hold values from -6 to 6
- slot_wavenumber: int32 [512], replicated, may hold values from 0 to 511, each once
- timescale: float32 [128], replicated, may hold values from 2 to 50
- lengthscale: float32 [128], replicated, may hold values from 128 to 512
Outputs:
- new_state: float32 [512, 2, 128, 512], P('lat', None, None, 'scale')
- pattern: float32 [128, 1536, 3072], P('scale', 'lat')
The draws below stay inside these ranges and needn't reach their ends.
Inputs may be any that keep to these rules, and one draw needn't show every extreme that they name: `slot_wavenumber`: each wavenumber 0 to 511 stands in exactly one slot.
All inputs are finite; a program needn't handle non-finite values.
Results may differ from the reference program's by a relative error of at most 0.0069.
Values may be sent and summed in bfloat16 or wider, within the bound.
A program may use at most 448 MiB of HBM per device.

```python
import math
import jax
import jax.numpy as jnp
from jax import lax

M = 512
NLAT = 1536
NLON = 3072
FIELDS = 128


def block_scale(key, dims, cuts, low, top_value):
    def one(position, shards_of):
        heights = jax.random.uniform(jax.random.fold_in(jax.random.fold_in(key, 6), position), (shards_of,), jnp.float32, low / len(cuts), top_value / len(cuts))
        return jnp.repeat(jnp.exp(heights), dims[position] // shards_of).reshape((-1,) + (1,) * (len(dims) - position - 1))

    loudness = one(*cuts[0])
    for cut in cuts[1:]:
        loudness = loudness * one(*cut)
    return loudness


def gaussian(own_key, extent, spread, most, shards=(), kind=jnp.bfloat16):
    level = block_scale(own_key, extent, shards, -0.22, 0.18) if shards else 1.0
    result = jax.random.normal(own_key, extent, jnp.float32) * spread * level
    return jnp.minimum(jnp.maximum(result, -most), most).astype(kind)


def setup_inputs(seed: int = 0) -> dict:
    streams_of = jax.random.split(jax.random.key(seed), 6)
    return {
        "state": gaussian(streams_of[0], (M, 2, FIELDS, M), 1.0, 6.0, ((0, 8), (3, 4)), jnp.float32),
        "noise": gaussian(streams_of[1], (M, 2, FIELDS, M), 1.0, 6.0, ((0, 8), (3, 4)), jnp.float32),
        "slot_wavenumber": jax.random.permutation(streams_of[2], M).astype(jnp.int32),
        "timescale": jnp.clip(jnp.exp(jax.random.uniform(streams_of[3], (FIELDS,), jnp.float32, math.log(2.0), math.log(50.0))), 2.0, 50.0),
        "lengthscale": jnp.clip(jnp.exp(jax.random.uniform(streams_of[4], (FIELDS,), jnp.float32, math.log(128.0), math.log(512.0))), 128.0, 512.0),
    }


log_floor = -60.0

def start_values(orders_local, sine_row):
    orders = orders_local.astype(jnp.float32)[:, None]
    log_head = 0.5 * (jax.scipy.special.gammaln(2.0 * orders + 1.0) + jnp.log(2.0 * orders + 1.0) - math.log(2.0)) - orders * math.log(2.0) - jax.scipy.special.gammaln(orders + 1.0)
    log_start = log_head + orders * jnp.log(sine_row)[None, :]
    return jnp.where(log_start >= log_floor, jnp.exp(jnp.maximum(log_start, log_floor)), 0.0)

def ratio(degree, orders):
    squared = degree * degree
    return jnp.sqrt(jnp.maximum(squared - orders * orders, 0.0) / (4.0 * squared - 1.0))

def next_row(degree, orders, cosine_row, pole_start, previous, earlier):
    ratio_here = ratio(degree, orders)
    ratio_before = ratio(degree - 1.0, orders)
    is_above = degree > orders
    grown_row = (cosine_row * previous - ratio_before * earlier) / jnp.where(is_above, ratio_here, 1.0)
    return jnp.where(degree == orders, pole_start, jnp.where(is_above, grown_row, 0.0))

def fourier_table(slot_wavenumber):
    points = jnp.arange(NLON).astype(jnp.int32)
    phase_index = slot_wavenumber[:, None] * points[None, :] % NLON
    angles = phase_index.astype(jnp.float32) * (2.0 * math.pi / NLON)
    weight = jnp.where(slot_wavenumber == 0, 1.0, 2.0) / M
    fourier = jnp.stack([weight[:, None] * jnp.cos(angles), -weight[:, None] * jnp.sin(angles)], axis=1)
    return fourier.astype(jnp.bfloat16)

def reference(state, noise, slot_wavenumber, timescale, lengthscale):
    decay_rate = jnp.exp(-1.0 / timescale)
    degrees = jnp.arange(M).astype(jnp.float32)
    amplitude = jnp.sqrt(1.0 - decay_rate * decay_rate)[:, None] * jnp.exp(-degrees[None, :] * (degrees[None, :] + 1.0) / (2.0 * lengthscale[:, None] ** 2)) * (M / lengthscale)[:, None]
    new_state = decay_rate[None, None, :, None] * state + amplitude[None, None] * noise
    spectra = new_state.astype(jnp.bfloat16)
    colatitude = (jnp.arange(NLAT).astype(jnp.float32) + 0.5) * (math.pi / NLAT)
    cosine_row = jnp.cos(colatitude)[None, :]
    sine_row = jnp.sin(colatitude)
    block_width = min(M, 64)

    def block(block_index):
        first_slot = (block_index * block_width).astype(jnp.int32)
        orders_local = lax.dynamic_slice_in_dim(slot_wavenumber, first_slot, block_width)
        block_coeff = lax.dynamic_slice_in_dim(spectra, first_slot, block_width, 0)
        orders = orders_local.astype(jnp.float32)[:, None]
        pole_start = start_values(orders_local, sine_row)
        zeros_row = jnp.zeros((block_width, NLAT), jnp.float32)

        def advance(recurrence, degree):
            previous, earlier = recurrence
            new_row = next_row(degree, orders, cosine_row, pole_start, previous, earlier)
            return ((new_row, previous), new_row)
        _, legendre = lax.scan(advance, (zeros_row, zeros_row), jnp.arange(M).astype(jnp.float32))
        legendre = legendre.astype(jnp.bfloat16)
        product = jnp.einsum('srfn,nsl->srfl', block_coeff.astype(jnp.float32), legendre.astype(jnp.float32))
        return product.astype(jnp.bfloat16)
    grid_spec = lax.map(block, jnp.arange(M // block_width).astype(jnp.int32))
    grid_spec = grid_spec.reshape(M, 2, FIELDS, NLAT)
    fourier = fourier_table(slot_wavenumber)
    pattern = jnp.einsum('srfl,srk->flk', grid_spec.astype(jnp.float32), fourier.astype(jnp.float32))
    return (new_state, pattern)
```

```python
import math

import jax
import jax.numpy as jnp
from jax import lax
from jax.experimental import pallas as pl
from jax.experimental.pallas import tpu as pltpu
from jax.sharding import PartitionSpec as P

M = 512
NLAT = 1536
NLON = 3072


log_floor = -60.0


def start_values(orders_local, sine_row):
    orders = orders_local.astype(jnp.float32)[:, None]
    log_head = (
        0.5
        * (
            jax.scipy.special.gammaln(2.0 * orders + 1.0)
            + jnp.log(2.0 * orders + 1.0)
            - math.log(2.0)
        )
        - orders * math.log(2.0)
        - jax.scipy.special.gammaln(orders + 1.0)
    )
    log_start = log_head + orders * jnp.log(sine_row)[None, :]
    return jnp.where(log_start >= log_floor, jnp.exp(jnp.maximum(log_start, log_floor)), 0.0)


def ratio(degree, orders):
    squared = degree * degree
    return jnp.sqrt(jnp.maximum(squared - orders * orders, 0.0) / (4.0 * squared - 1.0))


GROUP = 8
ROWS = 16
LANES = 128


def synthesis_kernel(
    orders_ref, sign_ref, cosine_ref, pole_ref, even_ref, flip_ref, spectra_ref, out_ref,
    table, inverse, before, rows
):
    degree_count = table.shape[1]
    half = table.shape[2]
    fields = spectra_ref.shape[1]
    orders = orders_ref[...]

    def coefficients(n, carry):
        degree = n.astype(jnp.float32)
        ratio_here = ratio(degree, orders)
        inverse[n] = jnp.where(degree > orders, 1.0 / jnp.where(degree > orders, ratio_here, 1.0), 0.0)
        before[n] = ratio(degree - 1.0, orders)
        return carry

    lax.fori_loop(0, degree_count, coefficients, 0)

    for tile in range(half // LANES):
        lanes = slice(tile * LANES, (tile + 1) * LANES)
        cosine = cosine_ref[:, lanes]
        pole = pole_ref[:, lanes]

        def advance(block, recurrence):
            previous, earlier = recurrence
            first = pl.multiple_of(block * ROWS, ROWS)
            for offset in range(ROWS):
                n = first + offset
                degree = n.astype(jnp.float32)
                grown = (cosine * previous - before[n] * earlier) * inverse[n]
                row = jnp.where(orders == degree, pole, grown)
                rows[offset] = row
                previous, earlier = row, previous
            for slot in range(GROUP):
                table[slot, pl.ds(first, ROWS), lanes] = rows[:, slot, :].astype(jnp.bfloat16)
            return previous, earlier

        zero = jnp.zeros((GROUP, LANES), jnp.float32)
        lax.fori_loop(0, degree_count // ROWS, advance, (zero, zero))

    def multiply(slot, carry):
        whole = spectra_ref[slot]
        even = whole * even_ref[...]
        odd = whole - even
        stacked = jnp.concatenate([even, odd], axis=0)
        product = jnp.dot(stacked, table[slot], preferred_element_type=jnp.float32)
        even_part = product[:fields]
        odd_part = product[fields:]
        out_ref[slot, :, :half] = (even_part + odd_part).astype(jnp.bfloat16)
        difference = even_part - odd_part
        for tile in range(half // LANES):
            part = difference[:, tile * LANES : (tile + 1) * LANES] * sign_ref[slot]
            turned = jnp.dot(
                part.astype(jnp.bfloat16), flip_ref[...], preferred_element_type=jnp.float32
            )
            end = 2 * half - tile * LANES
            out_ref[slot, :, end - LANES : end] = turned.astype(jnp.bfloat16)
        return carry

    lax.fori_loop(0, GROUP, multiply, 0)


def synthesize(spectra, orders_local, cosine, pole_start):
    slot_count, fields, degree_count = spectra.shape
    half = pole_start.shape[1]
    orders = jnp.broadcast_to(orders_local.astype(jnp.float32)[:, None], (slot_count, LANES))
    sign = jnp.where(orders_local % 2 == 0, 1.0, -1.0).astype(jnp.float32)
    sign = jnp.broadcast_to(sign[:, None, None], (slot_count, 1, LANES))
    cosine = jnp.broadcast_to(cosine[None], (GROUP, half))
    even = (jnp.arange(degree_count) % 2 == 0).astype(jnp.bfloat16)[None]
    flip = jnp.eye(LANES, dtype=jnp.bfloat16)[:, ::-1]
    return pl.pallas_call(
        synthesis_kernel,
        grid=(slot_count // GROUP,),
        in_specs=[
            pl.BlockSpec((GROUP, LANES), lambda g: (g, 0)),
            pl.BlockSpec((GROUP, 1, LANES), lambda g: (g, 0, 0)),
            pl.BlockSpec((GROUP, half), lambda g: (0, 0)),
            pl.BlockSpec((GROUP, half), lambda g: (g, 0)),
            pl.BlockSpec((1, degree_count), lambda g: (0, 0)),
            pl.BlockSpec((LANES, LANES), lambda g: (0, 0)),
            pl.BlockSpec((GROUP, fields, degree_count), lambda g: (g, 0, 0)),
        ],
        out_specs=pl.BlockSpec((GROUP, fields, 2 * half), lambda g: (g, 0, 0)),
        out_shape=jax.ShapeDtypeStruct((slot_count, fields, 2 * half), jnp.bfloat16),
        scratch_shapes=[
            pltpu.VMEM((GROUP, degree_count, half), jnp.bfloat16),
            pltpu.VMEM((degree_count, GROUP, LANES), jnp.float32),
            pltpu.VMEM((degree_count, GROUP, LANES), jnp.float32),
            pltpu.VMEM((ROWS, GROUP, LANES), jnp.float32),
        ],
        compiler_params=pltpu.CompilerParams(vmem_limit_bytes=40 * 2**20),
    )(orders, sign, cosine, pole_start, even, flip, spectra)


def fourier_table(slot_wavenumber):
    points = jnp.arange(NLON)
    phase_index = slot_wavenumber[:, None] * points[None, :] % NLON
    angles = phase_index.astype(jnp.float32) * (2.0 * math.pi / NLON)
    weight = jnp.where(slot_wavenumber == 0, 1.0, 2.0) / M
    fourier = jnp.stack(
        [weight[:, None] * jnp.cos(angles), -weight[:, None] * jnp.sin(angles)], axis=1
    )
    return fourier.astype(jnp.bfloat16)


def on_device(state, noise, slot_wavenumber, timescale, lengthscale):
    slot_count = state.shape[0]
    local_degrees = state.shape[3]
    scale_index = lax.axis_index("scale")
    blocks = lax.axis_size("scale")
    degrees = (scale_index * local_degrees + jnp.arange(local_degrees)).astype(jnp.float32)
    decay_rate = jnp.exp(-1.0 / timescale)
    amplitude = (
        jnp.sqrt(1.0 - decay_rate * decay_rate)[:, None]
        * jnp.exp(-degrees[None, :] * (degrees[None, :] + 1.0) / (2.0 * lengthscale[:, None] ** 2))
        * (M / lengthscale)[:, None]
    )
    new_state = decay_rate[None, None, :, None] * state + amplitude[None, None] * noise
    spectra_bf = new_state.astype(jnp.bfloat16)
    orders_local = lax.dynamic_slice_in_dim(
        slot_wavenumber, lax.axis_index("lat") * slot_count, slot_count
    )
    half = NLAT // 2
    colatitude = (jnp.arange(half).astype(jnp.float32) + 0.5) * (math.pi / NLAT)
    pole_start = start_values(orders_local, jnp.sin(colatitude))
    own_spectra = lax.all_to_all(spectra_bf, "scale", split_axis=2, concat_axis=3, tiled=True)
    own_fields = own_spectra.shape[2]
    grid_spec = synthesize(
        own_spectra.reshape(slot_count, 2 * own_fields, blocks * local_degrees),
        orders_local,
        jnp.cos(colatitude),
        pole_start,
    ).reshape(slot_count, 2, own_fields, NLAT)
    transposed_spec = lax.all_to_all(grid_spec, "lat", split_axis=3, concat_axis=0, tiled=True)
    fourier = fourier_table(slot_wavenumber)
    pattern = lax.dot_general(
        transposed_spec, fourier, (((0, 1), (0, 1)), ((), ())), preferred_element_type=jnp.float32
    )
    return (new_state, pattern)


def solution(mesh):
    placed = (P("lat", None, None, "scale"), P("lat", None, None, "scale"), P(), P(), P())
    return jax.shard_map(
        on_device,
        mesh=mesh,
        in_specs=placed,
        out_specs=(P("lat", None, None, "scale"), P("scale", "lat", None)),
        check_vma=False,
    )
```
